32 devices in a mesh: dp: 8 (over y, x, core), tensor: 4 (over z).
Axes of the slice: x: 2, y: 2, z: 4, core: 2. Of those that a mesh axis runs over, the one named last changes fastest.
Arguments:
- inputs: bfloat16 [1024, 8192], P('dp', 'tensor'), may hold values from -6 to 6
- cotangent: bfloat16 [1024, 8192], P('dp', 'tensor'), may hold values from -6 to 6
- w_first: bfloat16 [32, 256, 256], P('tensor'), may hold values from -0.375 to 0.375
- w_second: bfloat16 [32, 256, 896], P('tensor'), may hold values from -0.375 to 0.375
- w_third: bfloat16 [32, 896, 256], P('tensor'), may hold values from -0.1875 to 0.1875
- w_fourth: bfloat16 [32, 256, 256], P('tensor'), may hold values from -0.375 to 0.375
- route_up: int32 [8192], replicated, may hold values from 0 to 8191, as said below
- route_down: int32 [8192], replicated, may hold values from 0 to 8191, as said below
Outputs:
- layer_out: bfloat16 [1024, 8192], P('dp', 'tensor')
- grad_input: bfloat16 [1024, 8192], P('dp', 'tensor')
- grad_first: float32 [32, 256, 256], P('tensor', 'dp')
- grad_second: float32 [32, 256, 896], P('tensor', 'dp')
- grad_third: float32 [32, 896, 256], P('tensor', 'dp')
- grad_fourth: float32 [32, 256, 256], P('tensor', 'dp')
The draws below stay inside these ranges and needn't reach their ends.
Inputs may be any that keep to these rules, and one draw needn't show every extreme that they name: `route_up`: A permutation of 0 .. 8191. For every destination block b (positions b * 256 to (b + 1) * 256 - 1), its sources contain exactly 8 features of each of the 32 source blocks. `route_down`: same law as route_up, drawn independently.
All inputs are finite; a program needn't handle non-finite values.
Results may differ from the reference program's by a relative error of at most 0.011.
Values may be sent and summed in bfloat16 or wider, within the bound.
A program may use at most 128 MiB of HBM per device.

```python
import math
import jax
import jax.numpy as jnp
from jax import lax

D = 8192
H = 28672
NB = 32
TOK_DEV = 128
TOKENS = 1024


def monarch_route(key):
    width = D // NB
    share = width // NB
    key_src, key_dst = jax.random.split(key)
    sigma = jax.vmap(lambda k: jax.random.permutation(k, width))(jax.random.split(key_src, NB))
    tau = jax.vmap(lambda k: jax.random.permutation(k, width))(jax.random.split(key_dst, NB))
    picked = sigma.reshape(NB, NB, share).transpose(1, 0, 2)
    sources = (jnp.arange(NB, dtype=jnp.int32)[None, :, None] * width + picked).reshape(NB, width)
    inverse = jnp.argsort(tau, axis=1, stable=True)
    routed = jnp.take_along_axis(sources, inverse, axis=1)
    return routed.reshape(D).astype(jnp.int32)


def draw_route_up(key, part):
    key = jax.random.fold_in(key, 11)
    return monarch_route(key)


def draw_route_down(key, part):
    key = jax.random.fold_in(key, 29)
    return monarch_route(key)


def steps_of(own_key, dims, pieces, low, largest):
    factor_of, own = 1.0, jax.random.fold_in(own_key, 6)
    for axis_at, shards_of in pieces:
        steps = jnp.exp(jax.random.uniform(jax.random.fold_in(own, axis_at), (shards_of,), jnp.float32, low / len(pieces), largest / len(pieces)))
        factor_of = factor_of * jnp.repeat(steps, dims[axis_at] // shards_of).reshape([-1 if axis == axis_at else 1 for axis in range(len(dims))])
    return factor_of


def normal_values(key, dims, scale, reach, cuts=(), kind=jnp.bfloat16):
    values = jax.random.normal(key, dims, jnp.float32) * scale
    if len(cuts) > 0:
        values = steps_of(key, dims, cuts, -0.22, 0.18) * values
    return jnp.clip(values, min=-reach, max=reach).astype(kind)


def setup_inputs(seed: int = 0) -> dict:
    key_of = jax.random.split(jax.random.key(seed), 9)
    inputs = normal_values(key_of[0], (TOKENS, D), 1.0, 6.0, ((0, 8), (1, 4)))
    cotangent = normal_values(key_of[1], (TOKENS, D), 1.0, 6.0, ((0, 8), (1, 4)))
    w_first = normal_values(key_of[2], (NB, D // NB, D // NB), (D // NB) ** -0.5, 0.375, ((0, 4),))
    w_second = normal_values(key_of[3], (NB, D // NB, H // NB), (D // NB) ** -0.5, 0.375, ((0, 4),))
    w_third = normal_values(key_of[4], (NB, H // NB, D // NB), (H // NB) ** -0.5, 0.1875, ((0, 4),))
    w_fourth = normal_values(key_of[5], (NB, D // NB, D // NB), (D // NB) ** -0.5, 0.375, ((0, 4),))
    route_up = draw_route_up(jax.random.fold_in(key_of[8], 71), 0)
    route_down = draw_route_down(jax.random.fold_in(key_of[8], 71), 0)
    return {"inputs": inputs, "cotangent": cotangent, "w_first": w_first, "w_second": w_second, "w_third": w_third, "w_fourth": w_fourth, "route_up": route_up, "route_down": route_down}


def blocks(z, w):
    rows = z.shape[0]
    nb, fin, fout = w.shape
    out = jnp.einsum('tli,lio->tlo', z.reshape(rows, nb, fin).astype(jnp.float32), w.astype(jnp.float32))
    return out.reshape(rows, nb * fout)

def blocks_back(g, w):
    rows = g.shape[0]
    nb, fin, fout = w.shape
    out = jnp.einsum('tlo,lio->tli', g.reshape(rows, nb, fout).astype(jnp.float32), w.astype(jnp.float32))
    return out.reshape(rows, nb * fin)

def block_grad(z, g, nb, scale):
    rows = z.shape[0]
    left = z.reshape(rows, nb, -1).astype(jnp.float32)
    right = g.reshape(rows, nb, -1).astype(jnp.float32)
    return jnp.einsum('tli,tlo->lio', left, right) * scale

def gelu_tanh(v):
    return jax.nn.gelu(v, approximate=True)

def reference(inputs, cotangent, w_first, w_second, w_third, w_fourth, route_up, route_down):
    inv_up = jnp.argsort(route_up).astype(jnp.int32)
    inv_down = jnp.argsort(route_down).astype(jnp.int32)
    scale = 1.0 / math.sqrt(TOKENS)
    groups = inputs.shape[0] // TOK_DEV
    in_groups = inputs.reshape(groups, TOK_DEV, D)
    cot_groups = cotangent.reshape(groups, TOK_DEV, D)

    def rounded(term):
        return lax.optimization_barrier(term.astype(jnp.bfloat16)).astype(jnp.float32)

    def one_group(carry, pair):
        tokens, cot = pair
        first_act = blocks(tokens, w_first).astype(jnp.bfloat16)
        mixed_up = first_act[:, route_up]
        pre_act = blocks(mixed_up, w_second).astype(jnp.bfloat16)
        pre_float = pre_act.astype(jnp.float32)
        hidden_act = gelu_tanh(pre_float).astype(jnp.bfloat16)
        third_act = blocks(hidden_act, w_third).astype(jnp.bfloat16)
        mixed_down = third_act[:, route_down]
        layer_out = blocks(mixed_down, w_fourth).astype(jnp.bfloat16)
        back_mixed_down = blocks_back(cot, w_fourth).astype(jnp.bfloat16)
        back_third = back_mixed_down[:, inv_down]
        back_hidden = blocks_back(back_third, w_third)
        pull = jax.vjp(gelu_tanh, pre_float)[1]
        back_pre = pull(back_hidden)[0].astype(jnp.bfloat16)
        back_mixed_up = blocks_back(back_pre, w_second).astype(jnp.bfloat16)
        back_first = back_mixed_up[:, inv_up]
        grad_input = blocks_back(back_first, w_first).astype(jnp.bfloat16)
        terms = (block_grad(tokens, back_first, NB, scale), block_grad(mixed_up, back_pre, NB, scale), block_grad(hidden_act, back_third, NB, scale), block_grad(mixed_down, cot, NB, scale))
        carry = tuple((total + rounded(term) for total, term in zip(carry, terms)))
        return (carry, (layer_out, grad_input))
    start = (jnp.zeros(w_first.shape, jnp.float32), jnp.zeros(w_second.shape, jnp.float32), jnp.zeros(w_third.shape, jnp.float32), jnp.zeros(w_fourth.shape, jnp.float32))
    sums, outs = lax.scan(one_group, start, (in_groups, cot_groups))
    layer_out = outs[0].reshape(groups * TOK_DEV, D)
    grad_input = outs[1].reshape(groups * TOK_DEV, D)
    return (layer_out, grad_input, sums[0], sums[1], sums[2], sums[3])
```

```python
import functools
import math

import jax
import jax.numpy as jnp
from jax import lax
from jax.experimental import pallas as pl
from jax.experimental.pallas import tpu as pltpu
from jax.sharding import PartitionSpec as P


def blocks(z, w):
    rows = z.shape[0]
    nblk, fin, fout = w.shape
    out = jnp.einsum(
        "tli,lio->tlo", z.reshape(rows, nblk, fin), w, preferred_element_type=jnp.float32
    )
    return out.reshape(rows, nblk * fout)


def blocks_back(g, w):
    rows = g.shape[0]
    nblk, fin, fout = w.shape
    out = jnp.einsum(
        "tlo,lio->tli", g.reshape(rows, nblk, fout), w, preferred_element_type=jnp.float32
    )
    return out.reshape(rows, nblk * fin)


def block_grad(z, g, nblk, scale):
    rows = z.shape[0]
    total = jnp.einsum(
        "tli,tlo->lio",
        z.reshape(rows, nblk, -1),
        g.reshape(rows, nblk, -1),
        preferred_element_type=jnp.float32,
    )
    return total * scale


def gelu_tanh(v):
    return jax.nn.gelu(v, approximate=True)


def route_tables(route_all, width, ranks, rank):
    pieces = width // ranks
    grid = route_all.reshape(ranks, width)
    owner = grid // width
    local_col = grid - owner * width
    owner_hot = owner[:, :, None] == jnp.arange(ranks, dtype=jnp.int32)[None, None, :]
    counted = jnp.cumsum(owner_hot.astype(jnp.int32), axis=1)
    position = jnp.sum(jnp.where(owner_hot, counted, 0), axis=2) - 1
    recv_slot = owner * pieces + position
    my_slots = lax.dynamic_index_in_dim(recv_slot, rank, axis=0, keepdims=False)
    lanes = jnp.arange(width, dtype=jnp.int32)
    place_mat = (lanes[:, None] == my_slots[None, :]).astype(jnp.bfloat16)
    send_slot = (jnp.arange(ranks, dtype=jnp.int32)[:, None] * pieces + position).reshape(-1)
    owned = (owner == rank).reshape(-1)
    flat_col = local_col.reshape(-1)
    picks = jnp.logical_and(owned[None, :], send_slot[None, :] == lanes[:, None])
    col_of_slot = jnp.sum(jnp.where(picks, flat_col[None, :], 0), axis=1)
    send_mat = (lanes[:, None] == col_of_slot[None, :]).astype(jnp.bfloat16)
    return (send_mat, place_mat)


def apply_perm(x, table):
    return jnp.dot(x, table, preferred_element_type=jnp.float32).astype(jnp.bfloat16)


def apply_back(x, table):
    return lax.dot_general(
        x, table, (((1,), (1,)), ((), ())), preferred_element_type=jnp.float32
    ).astype(jnp.bfloat16)


def body(inputs, cotangent, w_first, w_second, w_third, w_fourth, route_up, route_down):
    ranks = lax.axis_size("tensor")
    rank = lax.axis_index("tensor")
    tok = inputs.shape[0]
    width = inputs.shape[1]
    pieces = width // ranks
    nblk = w_first.shape[0]
    scale = 1.0 / math.sqrt(tok * lax.axis_size("dp"))
    up_send, up_place = route_tables(route_up, width, ranks, rank)
    down_send, down_place = route_tables(route_down, width, ranks, rank)
    first_act = blocks(inputs, w_first).astype(jnp.bfloat16)
    outgoing = apply_perm(first_act, up_send).reshape(tok, ranks, pieces)
    received = lax.all_to_all(outgoing, "tensor", split_axis=1, concat_axis=1, tiled=True)
    mixed = apply_perm(received.reshape(received.shape[0], width), up_place)
    mixed_up = mixed
    pre_act = blocks(mixed, w_second).astype(jnp.bfloat16)
    pre_float = pre_act.astype(jnp.float32)
    hidden_act = gelu_tanh(pre_float).astype(jnp.bfloat16)
    third_act = blocks(hidden_act, w_third).astype(jnp.bfloat16)
    outgoing = apply_perm(third_act, down_send).reshape(tok, ranks, pieces)
    received = lax.all_to_all(outgoing, "tensor", split_axis=1, concat_axis=1, tiled=True)
    mixed = apply_perm(received.reshape(received.shape[0], width), down_place)
    layer_out = blocks(mixed, w_fourth).astype(jnp.bfloat16)
    back_mixed_down = blocks_back(cotangent, w_fourth).astype(jnp.bfloat16)
    grad_fourth = block_grad(mixed, cotangent, nblk, scale)
    returning = apply_back(back_mixed_down, down_place).reshape(tok, ranks, pieces)
    received = lax.all_to_all(returning, "tensor", split_axis=1, concat_axis=1, tiled=True)
    back = apply_back(received.reshape(received.shape[0], width), down_send)
    back_third = back
    back_hidden = blocks_back(back, w_third)
    grad_third = block_grad(hidden_act, back_third, nblk, scale)
    pull = jax.vjp(gelu_tanh, pre_float)[1]
    back_pre = pull(back_hidden)[0].astype(jnp.bfloat16)
    grad_second = block_grad(mixed_up, back_pre, nblk, scale)
    back_mixed_up = blocks_back(back_pre, w_second).astype(jnp.bfloat16)
    returning = apply_back(back_mixed_up, up_place).reshape(tok, ranks, pieces)
    received = lax.all_to_all(returning, "tensor", split_axis=1, concat_axis=1, tiled=True)
    back = apply_back(received.reshape(received.shape[0], width), up_send)
    grad_input = blocks_back(back, w_first).astype(jnp.bfloat16)
    grad_first = block_grad(inputs, back, nblk, scale)
    def shared(total):
        return lax.psum_scatter(
            total.astype(jnp.bfloat16), "dp", scatter_dimension=1, tiled=True
        ).astype(jnp.float32)

    return (
        layer_out, grad_input, shared(grad_first), shared(grad_second),
        shared(grad_third), shared(grad_fourth),
    )


MESH = pl.DeviceIdType.MESH
NN = (((1,), (0,)), ((), ()))
NT = (((1,), (1,)), ((), ()))
TN = (((0,), (0,)), ((), ()))
GELU_C = 0.7978845608
GELU_A = 0.044715


def mm(a, b, dims):
    return lax.dot_general(a, b, dims, preferred_element_type=jnp.float32)


def route_slots(routes, nb, ranks, rank):
    bw = routes.shape[-1]
    share = bw // nb
    nblk = nb // ranks
    src = routes // bw
    col = routes - src * bw
    hot = src[:, :, None, :] == jnp.arange(nb, dtype=jnp.int32)[None, None, :, None]
    upto = jnp.arange(bw)[:, None] <= jnp.arange(bw)[None, :]
    counted = jnp.einsum(
        "zbsk,kl->zbsl",
        hot.astype(jnp.bfloat16),
        upto.astype(jnp.bfloat16),
        preferred_element_type=jnp.float32,
    )
    j = jnp.sum(jnp.where(hot, counted, 0.0), axis=2).astype(jnp.int32) - 1
    slot = src * share + j
    mine = lax.dynamic_slice_in_dim(slot, rank * nblk, nblk, 1)
    local = slot - rank * (nblk * share)
    m = jnp.arange(nblk * share, dtype=jnp.int32)[None, None, :, None]
    cols = jnp.sum(jnp.where(local[:, :, None, :] == m, col[:, :, None, :], 0), axis=3)
    cols = cols.reshape(2, nb, nblk, share).transpose(0, 1, 3, 2).reshape(2, bw, nblk)
    return mine, cols


def layer_kernel(ranks, nblk, tok, bw, hw, scale, inp, cot, w1, w2, w3, w4, slot, cols,
                 out, gin, o1, o2, o3, o4,
                 pmat, smat, act, mup, mdn, bth, bfs, pre, hid, bpr, stage, sbuf, rbuf,
                 g1, g2, g3, g4, a1, a2, a3, a4, b1, b2, b3, b4, c1, c2, c3, c4,
                 ssem, rsem, asend, arecv, bsend, brecv, csend, crecv):
    bf = jnp.bfloat16
    rank = lax.axis_index("tensor")
    dp = lax.axis_index("dp")
    core = dp % 2
    x = (dp // 2) % 2
    y = dp // 4
    to_core = dp + 1 - 2 * core
    to_x = dp + 2 - 4 * x
    to_y = dp + 4 - 8 * y
    share = bw // (nblk * ranks)
    part = nblk * share
    half = nblk // 2
    gs, ras, rbs, rcs, outs = (g1, g2, g3, g4), (a1, a2, a3, a4), (b1, b2, b3, b4), (c1, c2, c3, c4), (o1, o2, o3, o4)

    barrier = pltpu.get_barrier_semaphore()
    for k in range(1, ranks):
        pl.semaphore_signal(barrier, inc=1, device_id=(dp, (rank + k) % ranks), device_id_type=MESH)
    for peer in (to_core, to_x, to_y):
        pl.semaphore_signal(barrier, inc=1, device_id=(peer, rank), device_id_type=MESH)

    lane = lax.broadcasted_iota(jnp.int32, (bw, bw), 1)
    row = lax.broadcasted_iota(jnp.int32, (bw, bw), 0)

    def make_smat(z):
        for s in range(nblk):
            smat[z, s] = (cols[z, :, s:s + 1] == lane).astype(jnp.float32).astype(bf)

    def make_pmat(z):
        for d in range(nblk):
            pmat[z, d] = (slot[z, d:d + 1, :] == row).astype(jnp.float32).astype(bf)

    def blk(b):
        return pl.ds(pl.multiple_of(b * bw, bw), bw)

    def each(step):
        def one(b, carry):
            step(b)
            return carry
        lax.fori_loop(0, nblk, one, 0)

    def hop(e, k):
        peer = (rank + k) % ranks
        return pltpu.make_async_remote_copy(
            src_ref=sbuf.at[e, peer], dst_ref=rbuf.at[e, rank],
            send_sem=ssem.at[e, k - 1], recv_sem=rsem.at[e, k - 1],
            device_id=(dp, peer), device_id_type=MESH)

    def send(e):
        for k in (2, 1, 3) if ranks == 4 else range(1, ranks):
            hop(e, k).start()
        rbuf[e, rank] = sbuf[e, rank]

    def arrive(e):
        for k in range(1, ranks):
            hop(e, k).wait_recv()

    def sort_out(z, b, value):
        rows = mm(smat[z, b], value, NT).reshape(ranks, nblk, share, tok)
        stage[:, :, pl.ds(pl.multiple_of(b * share, share), share), :] = rows

    def send_sorted(e):
        sbuf[e] = stage[...].astype(bf)
        send(e)

    def placed(e, z, b):
        return mm(rbuf[e, :, b].reshape(bw, tok), pmat[z, b], TN).astype(bf)

    def unplace(e, z, b, value):
        sbuf[e, :, b] = mm(pmat[z, b], value, NT).astype(bf).reshape(ranks, part, tok)

    def unsorted(z, b):
        rows = stage[:, :, pl.ds(pl.multiple_of(b * share, share), share), :]
        return mm(rows.reshape(bw, tok).astype(bf), smat[z, b], TN).astype(bf)

    def put_grad(w, b, left, right):
        term = (mm(left, right, TN) * scale).astype(bf)
        gs[w][:, :, :, b] = term.reshape((2, 2, 2) + gs[w].shape[4:])

    def copy_a(w):
        return pltpu.make_async_remote_copy(
            src_ref=gs[w].at[:, :, 1 - core], dst_ref=ras[w],
            send_sem=asend.at[w], recv_sem=arecv.at[w],
            device_id=(to_core, rank), device_id_type=MESH)

    lo, hi = pl.ds(0, half), pl.ds(half, half)

    def copies_b(w):
        return (
            pltpu.make_async_remote_copy(
                src_ref=ras[w].at[:, 1 - x, lo], dst_ref=rbs[w].at[:, lo],
                send_sem=bsend.at[w, 0], recv_sem=brecv.at[w, 0],
                device_id=(to_x, rank), device_id_type=MESH),
            pltpu.make_async_remote_copy(
                src_ref=ras[w].at[1 - y, :, hi], dst_ref=rbs[w].at[:, hi],
                send_sem=bsend.at[w, 1], recv_sem=brecv.at[w, 1],
                device_id=(to_y, rank), device_id_type=MESH))

    def copies_c(w):
        return (
            pltpu.make_async_remote_copy(
                src_ref=rbs[w].at[1 - y, lo], dst_ref=rcs[w].at[lo],
                send_sem=csend.at[w, 0], recv_sem=crecv.at[w, 0],
                device_id=(to_y, rank), device_id_type=MESH),
            pltpu.make_async_remote_copy(
                src_ref=rbs[w].at[1 - x, hi], dst_ref=rcs[w].at[hi],
                send_sem=csend.at[w, 1], recv_sem=crecv.at[w, 1],
                device_id=(to_x, rank), device_id_type=MESH))

    def f32(v):
        return v.astype(jnp.float32)

    def a_to_b(w):
        copy_a(w).wait_recv()

        def step(b):
            ras[w][:, :, b] = (f32(ras[w][:, :, b]) + f32(gs[w][:, :, core, b])).astype(bf)
        each(step)
        for c in copies_b(w):
            c.start()

    def b_to_c(w):
        for c in copies_b(w):
            c.wait_recv()

        def one(b, carry):
            rbs[w][:, b] = (f32(rbs[w][:, b]) + f32(ras[w][:, x, b])).astype(bf)
            rbs[w][:, b + half] = (f32(rbs[w][:, b + half]) + f32(ras[w][y, :, b + half])).astype(bf)
            return carry
        lax.fori_loop(0, half, one, 0)
        for c in copies_c(w):
            c.start()

    def finish(w):
        for c in copies_c(w):
            c.wait_recv()

        def one(b, carry):
            outs[w][b] = f32(rbs[w][y, b]) + f32(rcs[w][b])
            outs[w][b + half] = f32(rbs[w][x, b + half]) + f32(rcs[w][b + half])
            return carry
        lax.fori_loop(0, half, one, 0)

    make_smat(0)

    def first(b):
        sort_out(0, b, mm(inp[:, blk(b)], w1[b], NN).astype(bf))
    each(first)
    pl.semaphore_wait(barrier, ranks - 1 + 3)
    send_sorted(0)

    make_pmat(1)

    def back_fourth(b):
        unplace(1, 1, b, mm(cot[:, blk(b)], w4[b], NT).astype(bf))
    each(back_fourth)
    send(1)
    make_pmat(0)
    make_smat(1)

    arrive(0)

    def middle(b):
        m = placed(0, 0, b)
        mup[b] = m
        p = mm(m, w2[b], NN).astype(bf)
        pre[b] = p
        v = f32(p)
        h = (0.5 * v * (1.0 + jnp.tanh(GELU_C * (v + GELU_A * (v * v * v))))).astype(bf)
        hid[b] = h
        sort_out(1, b, mm(h, w3[b], NN).astype(bf))
    each(middle)
    send_sorted(2)

    arrive(1)
    stage[...] = f32(rbuf[1])

    def third(b):
        t = unsorted(1, b)
        bth[b] = t
        put_grad(2, b, hid[b], t)
    each(third)
    copy_a(2).start()

    def back_second(b):
        v = f32(pre[b])
        v2 = v * v
        th = jnp.tanh(GELU_C * (v + GELU_A * (v2 * v)))
        slope = 0.5 * (1.0 + th) + 0.5 * v * (1.0 - th * th) * (GELU_C * (1.0 + 3.0 * GELU_A * v2))
        p = (mm(bth[b], w3[b], NT) * slope).astype(bf)
        bpr[b] = p
        unplace(3, 0, b, mm(p, w2[b], NT).astype(bf))
    each(back_second)
    send(3)

    a_to_b(2)

    def second(b):
        put_grad(1, b, mup[b], bpr[b])
    each(second)
    copy_a(1).start()

    arrive(2)

    def fourth(b):
        m = placed(2, 1, b)
        out[:, blk(b)] = mm(m, w4[b], NN).astype(bf)
        put_grad(3, b, m, cot[:, blk(b)])
    each(fourth)
    copy_a(3).start()
    a_to_b(1)
    a_to_b(3)

    arrive(3)
    stage[...] = f32(rbuf[3])

    def last(b):
        t = unsorted(0, b)
        put_grad(0, b, inp[:, blk(b)], t)
        gin[:, blk(b)] = mm(t, w1[b], NT).astype(bf)
    each(last)
    copy_a(0).start()
    a_to_b(0)
    for w in (2, 1, 3, 0):
        b_to_c(w)
    for w in (2, 1, 3, 0):
        finish(w)

    for e in range(4):
        for k in range(1, ranks):
            hop(e, k).wait_send()
    for w in range(4):
        copy_a(w).wait_send()
        for c in copies_b(w) + copies_c(w):
            c.wait_send()


def fused_body(inputs, cotangent, w_first, w_second, w_third, w_fourth, route_up, route_down):
    ranks = lax.axis_size("tensor")
    dps = lax.axis_size("dp")
    rank = lax.axis_index("tensor")
    tok, width = inputs.shape
    nblk, bw, hw = w_second.shape
    nb = nblk * ranks
    part = bw // ranks
    scale = 1.0 / math.sqrt(tok * dps)
    routes = jnp.stack([route_up, route_down]).reshape(2, nb, bw)
    slot, cols = route_slots(routes, nb, ranks, rank)
    weights = (w_first, w_second, w_third, w_fourth)
    shapes = [(w.shape[1] // dps, w.shape[2]) for w in weights]
    bf = jnp.bfloat16
    vm = pltpu.VMEM
    scratch = [
        vm((2, nblk, bw, bw), bf), vm((2, nblk, bw, bw), bf),
        vm((nblk, tok, bw), bf), vm((nblk, tok, bw), bf), vm((nblk, tok, bw), bf),
        vm((nblk, tok, bw), bf), vm((nblk, tok, bw), bf),
        vm((nblk, tok, hw), bf), vm((nblk, tok, hw), bf), vm((nblk, tok, hw), bf),
        vm((ranks, nblk, part, tok), jnp.float32),
        vm((4, ranks, nblk, part, tok), bf), vm((4, ranks, nblk, part, tok), bf),
    ]
    scratch += [vm((2, 2, 2, nblk) + s, bf) for s in shapes]
    scratch += [vm((2, 2, nblk) + s, bf) for s in shapes]
    scratch += [vm((2, nblk) + s, bf) for s in shapes]
    scratch += [vm((nblk,) + s, bf) for s in shapes]
    dma = pltpu.SemaphoreType.DMA
    scratch += [dma((4, ranks - 1)), dma((4, ranks - 1)), dma((4,)), dma((4,))]
    scratch += [dma((4, 2))] * 4
    out_shape = [jax.ShapeDtypeStruct((tok, width), bf)] * 2
    out_shape += [jax.ShapeDtypeStruct((nblk,) + s, jnp.float32) for s in shapes]
    spec = pl.BlockSpec(memory_space=pltpu.VMEM)
    return tuple(pl.pallas_call(
        functools.partial(layer_kernel, ranks, nblk, tok, bw, hw, scale),
        out_shape=out_shape,
        in_specs=[spec] * 8,
        out_specs=[spec] * 6,
        scratch_shapes=scratch,
        compiler_params=pltpu.CompilerParams(
            collective_id=0, has_side_effects=True, vmem_limit_bytes=60 * 1024 * 1024),
    )(inputs, cotangent, *weights, slot, cols))


def solution(mesh):
    def pick(*args):
        inputs, w_first, w_third = args[0], args[2], args[4]
        ranks, dps = mesh.shape["tensor"], mesh.shape["dp"]
        nblk, bw = w_first.shape[:2]
        aligned = (
            dps == 8 and nblk % 2 == 0 and bw // (nblk * ranks) == 8
            and (bw // dps) % 16 == 0 and (w_third.shape[1] // dps) % 16 == 0
            and (bw // ranks) % 16 == 0 and inputs.shape[0] % 128 == 0
        )
        return (fused_body if aligned else body)(*args)

    return jax.shard_map(
        pick,
        mesh=mesh,
        in_specs=(
            P("dp", "tensor"),
            P("dp", "tensor"),
            P("tensor", None, None),
            P("tensor", None, None),
            P("tensor", None, None),
            P("tensor", None, None),
            P(),
            P(),
        ),
        out_specs=(
            P("dp", "tensor"),
            P("dp", "tensor"),
            P("tensor", "dp", None),
            P("tensor", "dp", None),
            P("tensor", "dp", None),
            P("tensor", "dp", None),
        ),
        check_vma=False,
    )
```

```python
import functools
import math

import jax
import jax.numpy as jnp
from jax import lax
from jax.experimental import pallas as pl
from jax.experimental.pallas import tpu as pltpu
from jax.sharding import PartitionSpec as P


def blocks(z, w):
    rows = z.shape[0]
    nblk, fin, fout = w.shape
    out = jnp.einsum(
        "tli,lio->tlo", z.reshape(rows, nblk, fin), w, preferred_element_type=jnp.float32
    )
    return out.reshape(rows, nblk * fout)


def blocks_back(g, w):
    rows = g.shape[0]
    nblk, fin, fout = w.shape
    out = jnp.einsum(
        "tlo,lio->tli", g.reshape(rows, nblk, fout), w, preferred_element_type=jnp.float32
    )
    return out.reshape(rows, nblk * fin)


def block_grad(z, g, nblk, scale):
    rows = z.shape[0]
    total = jnp.einsum(
        "tli,tlo->lio",
        z.reshape(rows, nblk, -1),
        g.reshape(rows, nblk, -1),
        preferred_element_type=jnp.float32,
    )
    return total * scale


def gelu_tanh(v):
    return jax.nn.gelu(v, approximate=True)


def route_tables(route_all, width, ranks, rank):
    pieces = width // ranks
    grid = route_all.reshape(ranks, width)
    owner = grid // width
    local_col = grid - owner * width
    owner_hot = owner[:, :, None] == jnp.arange(ranks, dtype=jnp.int32)[None, None, :]
    counted = jnp.cumsum(owner_hot.astype(jnp.int32), axis=1)
    position = jnp.sum(jnp.where(owner_hot, counted, 0), axis=2) - 1
    recv_slot = owner * pieces + position
    my_slots = lax.dynamic_index_in_dim(recv_slot, rank, axis=0, keepdims=False)
    lanes = jnp.arange(width, dtype=jnp.int32)
    place_mat = (lanes[:, None] == my_slots[None, :]).astype(jnp.bfloat16)
    send_slot = (jnp.arange(ranks, dtype=jnp.int32)[:, None] * pieces + position).reshape(-1)
    owned = (owner == rank).reshape(-1)
    flat_col = local_col.reshape(-1)
    picks = jnp.logical_and(owned[None, :], send_slot[None, :] == lanes[:, None])
    col_of_slot = jnp.sum(jnp.where(picks, flat_col[None, :], 0), axis=1)
    send_mat = (lanes[:, None] == col_of_slot[None, :]).astype(jnp.bfloat16)
    return (send_mat, place_mat)


def apply_perm(x, table):
    return jnp.dot(x, table, preferred_element_type=jnp.float32).astype(jnp.bfloat16)


def apply_back(x, table):
    return lax.dot_general(
        x, table, (((1,), (1,)), ((), ())), preferred_element_type=jnp.float32
    ).astype(jnp.bfloat16)


def body(inputs, cotangent, w_first, w_second, w_third, w_fourth, route_up, route_down):
    ranks = lax.axis_size("tensor")
    rank = lax.axis_index("tensor")
    tok = inputs.shape[0]
    width = inputs.shape[1]
    pieces = width // ranks
    nblk = w_first.shape[0]
    scale = 1.0 / math.sqrt(tok * lax.axis_size("dp"))
    up_send, up_place = route_tables(route_up, width, ranks, rank)
    down_send, down_place = route_tables(route_down, width, ranks, rank)
    first_act = blocks(inputs, w_first).astype(jnp.bfloat16)
    outgoing = apply_perm(first_act, up_send).reshape(tok, ranks, pieces)
    received = lax.all_to_all(outgoing, "tensor", split_axis=1, concat_axis=1, tiled=True)
    mixed = apply_perm(received.reshape(received.shape[0], width), up_place)
    mixed_up = mixed
    pre_act = blocks(mixed, w_second).astype(jnp.bfloat16)
    pre_float = pre_act.astype(jnp.float32)
    hidden_act = gelu_tanh(pre_float).astype(jnp.bfloat16)
    third_act = blocks(hidden_act, w_third).astype(jnp.bfloat16)
    outgoing = apply_perm(third_act, down_send).reshape(tok, ranks, pieces)
    received = lax.all_to_all(outgoing, "tensor", split_axis=1, concat_axis=1, tiled=True)
    mixed = apply_perm(received.reshape(received.shape[0], width), down_place)
    layer_out = blocks(mixed, w_fourth).astype(jnp.bfloat16)
    back_mixed_down = blocks_back(cotangent, w_fourth).astype(jnp.bfloat16)
    grad_fourth = block_grad(mixed, cotangent, nblk, scale)
    returning = apply_back(back_mixed_down, down_place).reshape(tok, ranks, pieces)
    received = lax.all_to_all(returning, "tensor", split_axis=1, concat_axis=1, tiled=True)
    back = apply_back(received.reshape(received.shape[0], width), down_send)
    back_third = back
    back_hidden = blocks_back(back, w_third)
    grad_third = block_grad(hidden_act, back_third, nblk, scale)
    pull = jax.vjp(gelu_tanh, pre_float)[1]
    back_pre = pull(back_hidden)[0].astype(jnp.bfloat16)
    grad_second = block_grad(mixed_up, back_pre, nblk, scale)
    back_mixed_up = blocks_back(back_pre, w_second).astype(jnp.bfloat16)
    returning = apply_back(back_mixed_up, up_place).reshape(tok, ranks, pieces)
    received = lax.all_to_all(returning, "tensor", split_axis=1, concat_axis=1, tiled=True)
    back = apply_back(received.reshape(received.shape[0], width), up_send)
    grad_input = blocks_back(back, w_first).astype(jnp.bfloat16)
    grad_first = block_grad(inputs, back, nblk, scale)
    def shared(total):
        return lax.psum_scatter(
            total.astype(jnp.bfloat16), "dp", scatter_dimension=1, tiled=True
        ).astype(jnp.float32)

    return (
        layer_out, grad_input, shared(grad_first), shared(grad_second),
        shared(grad_third), shared(grad_fourth),
    )


MESH = pl.DeviceIdType.MESH
NN = (((1,), (0,)), ((), ()))
NT = (((1,), (1,)), ((), ()))
TN = (((0,), (0,)), ((), ()))
GELU_C = 0.7978845608
GELU_A = 0.044715


def mm(a, b, dims):
    return lax.dot_general(a, b, dims, preferred_element_type=jnp.float32)


def route_slots(routes, nb, ranks, rank):
    bw = routes.shape[-1]
    share = bw // nb
    nblk = nb // ranks
    src = routes // bw
    col = routes - src * bw
    hot = src[:, :, None, :] == jnp.arange(nb, dtype=jnp.int32)[None, None, :, None]
    upto = jnp.arange(bw)[:, None] <= jnp.arange(bw)[None, :]
    counted = jnp.einsum(
        "zbsk,kl->zbsl",
        hot.astype(jnp.bfloat16),
        upto.astype(jnp.bfloat16),
        preferred_element_type=jnp.float32,
    )
    j = jnp.sum(jnp.where(hot, counted, 0.0), axis=2).astype(jnp.int32) - 1
    slot = src * share + j
    mine = lax.dynamic_slice_in_dim(slot, rank * nblk, nblk, 1)
    local = slot - rank * (nblk * share)
    m = jnp.arange(nblk * share, dtype=jnp.int32)[None, None, :, None]
    cols = jnp.sum(jnp.where(local[:, :, None, :] == m, col[:, :, None, :], 0), axis=3)
    cols = cols.reshape(2, nb, nblk, share).transpose(0, 1, 3, 2).reshape(2, bw, nblk)
    return mine, cols


def layer_kernel(ranks, nblk, tok, bw, hw, scale, inp, cot, w1, w2, w3, w4, slot, cols,
                 out, gin, o1, o2, o3, o4,
                 pmat, smat, act, mup, mdn, bth, bfs, pre, hid, bpr, stage, sbuf, rbuf,
                 g1, g2, g3, g4, a1, a2, a3, a4, b1, b2, b3, b4, c1, c2, c3, c4,
                 ssem, rsem, asend, arecv, bsend, brecv, csend, crecv):
    bf = jnp.bfloat16
    rank = lax.axis_index("tensor")
    dp = lax.axis_index("dp")
    core = dp % 2
    x = (dp // 2) % 2
    y = dp // 4
    to_core = dp + 1 - 2 * core
    to_x = dp + 2 - 4 * x
    to_y = dp + 4 - 8 * y
    share = bw // (nblk * ranks)
    part = nblk * share
    hb = nblk // 2
    quarter = hb // 2
    gs, ras, rbs, rcs, outs = (g1, g2, g3, g4), (a1, a2, a3, a4), (b1, b2, b3, b4), (c1, c2, c3, c4), (o1, o2, o3, o4)

    barrier = pltpu.get_barrier_semaphore()
    for k in range(1, ranks):
        pl.semaphore_signal(barrier, inc=1, device_id=(dp, (rank + k) % ranks), device_id_type=MESH)
    for peer in (to_core, to_x, to_y):
        pl.semaphore_signal(barrier, inc=1, device_id=(peer, rank), device_id_type=MESH)

    lane = lax.broadcasted_iota(jnp.int32, (bw, bw), 1)
    row = lax.broadcasted_iota(jnp.int32, (bw, bw), 0)

    def make_smat(z):
        for s in range(nblk):
            smat[z, s] = (cols[z, :, s:s + 1] == lane).astype(jnp.float32).astype(bf)

    def make_pmat(z):
        for d in range(nblk):
            pmat[z, d] = (slot[z, d:d + 1, :] == row).astype(jnp.float32).astype(bf)

    def blk(b):
        return pl.ds(pl.multiple_of(b * bw, bw), bw)

    def each(step, c=None):
        def one(b, carry):
            step(b)
            return carry
        lax.fori_loop(*((0, nblk) if c is None else (c * hb, c * hb + hb)), one, 0)

    def piece(e, c):
        if e in (0, 3):
            return pl.ds(c * hb, hb), slice(None)
        return slice(None), pl.ds(c * hb * share, hb * share)

    def hop(e, c, k):
        peer = (rank + k) % ranks
        rows, cut = piece(e, c)
        return pltpu.make_async_remote_copy(
            src_ref=sbuf.at[e, peer, rows, cut], dst_ref=rbuf.at[e, rank, rows, cut],
            send_sem=ssem.at[e, c, k - 1], recv_sem=rsem.at[e, c, k - 1],
            device_id=(dp, peer), device_id_type=MESH)

    def send(e, c):
        for k in (2, 1, 3) if ranks == 4 else range(1, ranks):
            hop(e, c, k).start()
        rows, cut = piece(e, c)
        rbuf[e, rank, rows, cut] = sbuf[e, rank, rows, cut]

    def arrive(e, c):
        for k in range(1, ranks):
            hop(e, c, k).wait_recv()

    def sort_out(z, b, value):
        rows = mm(smat[z, b], value, NT).reshape(ranks, nblk, share, tok)
        stage[:, :, pl.ds(pl.multiple_of(b * share, share), share), :] = rows

    def placed(e, z, b):
        return mm(rbuf[e, :, b].reshape(bw, tok), pmat[z, b], TN).astype(bf)

    def unplace(e, z, b, value):
        sbuf[e, :, b] = mm(pmat[z, b], value, NT).astype(bf).reshape(ranks, part, tok)

    def unsorted(z, b):
        rows = stage[:, :, pl.ds(pl.multiple_of(b * share, share), share), :]
        return mm(rows.reshape(bw, tok).astype(bf), smat[z, b], TN).astype(bf)

    def put_grad(w, b, left, right):
        term = (mm(left, right, TN) * scale).astype(bf)
        gs[w][:, :, :, b] = term.reshape((2, 2, 2) + gs[w].shape[4:])

    def copy_a(w, c):
        return pltpu.make_async_remote_copy(
            src_ref=gs[w].at[:, :, 1 - core, pl.ds(c * hb, hb)],
            dst_ref=ras[w].at[:, :, pl.ds(c * hb, hb)],
            send_sem=asend.at[w, c], recv_sem=arecv.at[w, c],
            device_id=(to_core, rank), device_id_type=MESH)

    def spans(c):
        return pl.ds(c * hb, quarter), pl.ds(c * hb + quarter, quarter)

    def copies_b(w, c):
        lo, hi = spans(c)
        return (
            pltpu.make_async_remote_copy(
                src_ref=ras[w].at[:, 1 - x, lo], dst_ref=rbs[w].at[:, lo],
                send_sem=bsend.at[w, c, 0], recv_sem=brecv.at[w, c, 0],
                device_id=(to_x, rank), device_id_type=MESH),
            pltpu.make_async_remote_copy(
                src_ref=ras[w].at[1 - y, :, hi], dst_ref=rbs[w].at[:, hi],
                send_sem=bsend.at[w, c, 1], recv_sem=brecv.at[w, c, 1],
                device_id=(to_y, rank), device_id_type=MESH))

    def copies_c(w, c):
        lo, hi = spans(c)
        return (
            pltpu.make_async_remote_copy(
                src_ref=rbs[w].at[1 - y, lo], dst_ref=rcs[w].at[lo],
                send_sem=csend.at[w, c, 0], recv_sem=crecv.at[w, c, 0],
                device_id=(to_y, rank), device_id_type=MESH),
            pltpu.make_async_remote_copy(
                src_ref=rbs[w].at[1 - x, hi], dst_ref=rcs[w].at[hi],
                send_sem=csend.at[w, c, 1], recv_sem=crecv.at[w, c, 1],
                device_id=(to_x, rank), device_id_type=MESH))

    def f32(v):
        return v.astype(jnp.float32)

    def a_to_b(w, c):
        copy_a(w, c).wait_recv()

        def step(b):
            ras[w][:, :, b] = (f32(ras[w][:, :, b]) + f32(gs[w][:, :, core, b])).astype(bf)
        each(step, c)
        for copy in copies_b(w, c):
            copy.start()

    def b_to_c(w, c):
        for copy in copies_b(w, c):
            copy.wait_recv()

        def one(b, carry):
            rbs[w][:, b] = (f32(rbs[w][:, b]) + f32(ras[w][:, x, b])).astype(bf)
            h = b + quarter
            rbs[w][:, h] = (f32(rbs[w][:, h]) + f32(ras[w][y, :, h])).astype(bf)
            return carry
        lax.fori_loop(c * hb, c * hb + quarter, one, 0)
        for copy in copies_c(w, c):
            copy.start()

    def finish(w, c):
        for copy in copies_c(w, c):
            copy.wait_recv()

        def one(b, carry):
            h = b + quarter
            outs[w][b] = f32(rbs[w][y, b]) + f32(rcs[w][b])
            outs[w][h] = f32(rbs[w][x, h]) + f32(rcs[w][h])
            return carry
        lax.fori_loop(c * hb, c * hb + quarter, one, 0)

    make_smat(0)

    def first(b):
        sort_out(0, b, mm(inp[:, blk(b)], w1[b], NN).astype(bf))
    each(first)
    pl.semaphore_wait(barrier, ranks - 1 + 3)
    sbuf[0] = stage[...].astype(bf)
    send(0, 0)

    make_pmat(1)

    def back_fourth(b):
        unplace(1, 1, b, mm(cot[:, blk(b)], w4[b], NT).astype(bf))
    each(back_fourth)
    send(1, 0)
    make_pmat(0)
    make_smat(1)

    def middle(b):
        m = placed(0, 0, b)
        mup[b] = m
        p = mm(m, w2[b], NN).astype(bf)
        pre[b] = p
        v = f32(p)
        h = (0.5 * v * (1.0 + jnp.tanh(GELU_C * (v + GELU_A * (v * v * v))))).astype(bf)
        hid[b] = h
        sort_out(1, b, mm(h, w3[b], NN).astype(bf))
    def load(e, c):
        rows, cut = piece(e, c)
        stage[:, rows, cut] = f32(rbuf[e, :, rows, cut])

    def forward(c):
        each(middle, c)
        rows, cut = piece(2, c)
        sbuf[2, :, rows, cut] = stage[:, rows, cut].astype(bf)

    def third(b):
        t = unsorted(1, b)
        bth[b] = t
        put_grad(2, b, hid[b], t)

    def back_second(b):
        v = f32(pre[b])
        v2 = v * v
        th = jnp.tanh(GELU_C * (v + GELU_A * (v2 * v)))
        slope = 0.5 * (1.0 + th) + 0.5 * v * (1.0 - th * th) * (GELU_C * (1.0 + 3.0 * GELU_A * v2))
        p = (mm(bth[b], w3[b], NT) * slope).astype(bf)
        bpr[b] = p
        unplace(3, 0, b, mm(p, w2[b], NT).astype(bf))
    def second(b):
        put_grad(1, b, mup[b], bpr[b])

    def fourth(b):
        m = placed(2, 1, b)
        out[:, blk(b)] = mm(m, w4[b], NN).astype(bf)
        put_grad(3, b, m, cot[:, blk(b)])
    def last(b):
        t = unsorted(0, b)
        put_grad(0, b, inp[:, blk(b)], t)
        gin[:, blk(b)] = mm(t, w1[b], NT).astype(bf)

    arrive(0, 0)
    send(0, 1)
    forward(0)
    arrive(1, 0)
    send(1, 1)
    load(1, 0)
    each(third, 0)
    copy_a(2, 0).start()
    each(back_second, 0)
    a_to_b(2, 0)
    each(second, 0)
    copy_a(1, 0).start()

    arrive(0, 1)
    send(2, 0)
    forward(1)
    a_to_b(1, 0)
    arrive(1, 1)
    send(2, 1)
    send(3, 0)
    load(1, 1)
    each(third, 1)
    copy_a(2, 1).start()
    each(back_second, 1)
    send(3, 1)
    a_to_b(2, 1)
    each(second, 1)
    copy_a(1, 1).start()
    b_to_c(2, 0)
    a_to_b(1, 1)
    b_to_c(1, 0)

    for c in range(2):
        arrive(2, c)
    for c in range(2):
        each(fourth, c)
        copy_a(3, c).start()
    for c in range(2):
        a_to_b(3, c)
    b_to_c(2, 1)

    for c in range(2):
        arrive(3, c)
    stage[...] = f32(rbuf[3])
    for c in range(2):
        each(last, c)
        copy_a(0, c).start()
    for c in range(2):
        a_to_b(0, c)
    order = [(1, 1), (3, 0), (3, 1), (0, 0), (0, 1)]
    for w, c in order:
        b_to_c(w, c)
    for w, c in [(2, 0), (1, 0), (2, 1)] + order:
        finish(w, c)

    for c in range(2):
        for e in range(4):
            for k in range(1, ranks):
                hop(e, c, k).wait_send()
        for w in range(4):
            copy_a(w, c).wait_send()
            for copy in copies_b(w, c) + copies_c(w, c):
                copy.wait_send()


def hand_on(*refs):
    n = len(refs) // 2
    sem = refs[-1]
    copies = [
        pltpu.make_async_copy(refs[i], refs[n + i], sem.at[i]) for i in range(n)
    ]
    for copy in copies:
        copy.start()
    for copy in copies:
        copy.wait()


def fused_body(inputs, cotangent, w_first, w_second, w_third, w_fourth, route_up, route_down):
    ranks = lax.axis_size("tensor")
    dps = lax.axis_size("dp")
    rank = lax.axis_index("tensor")
    tok, width = inputs.shape
    nblk, bw, hw = w_second.shape
    nb = nblk * ranks
    part = bw // ranks
    scale = 1.0 / math.sqrt(tok * dps)
    routes = jnp.stack([route_up, route_down]).reshape(2, nb, bw)
    slot, cols = route_slots(routes, nb, ranks, rank)
    weights = (w_first, w_second, w_third, w_fourth)
    shapes = [(w.shape[1] // dps, w.shape[2]) for w in weights]
    bf = jnp.bfloat16
    vm = pltpu.VMEM
    scratch = [
        vm((2, nblk, bw, bw), bf), vm((2, nblk, bw, bw), bf),
        vm((nblk, tok, bw), bf), vm((nblk, tok, bw), bf), vm((nblk, tok, bw), bf),
        vm((nblk, tok, bw), bf), vm((nblk, tok, bw), bf),
        vm((nblk, tok, hw), bf), vm((nblk, tok, hw), bf), vm((nblk, tok, hw), bf),
        vm((ranks, nblk, part, tok), jnp.float32),
        vm((4, ranks, nblk, part, tok), bf), vm((4, ranks, nblk, part, tok), bf),
    ]
    scratch += [vm((2, 2, 2, nblk) + s, bf) for s in shapes]
    scratch += [vm((2, 2, nblk) + s, bf) for s in shapes]
    scratch += [vm((2, nblk) + s, bf) for s in shapes]
    scratch += [vm((nblk,) + s, bf) for s in shapes]
    dma = pltpu.SemaphoreType.DMA
    scratch += [dma((4, 2, ranks - 1))] * 2 + [dma((4, 2))] * 2
    scratch += [dma((4, 2, 2))] * 4
    out_shape = [jax.ShapeDtypeStruct((tok, width), bf)] * 2
    out_shape += [jax.ShapeDtypeStruct((nblk,) + s, jnp.float32) for s in shapes]
    spec = pl.BlockSpec(memory_space=pltpu.VMEM)
    results = pl.pallas_call(
        functools.partial(layer_kernel, ranks, nblk, tok, bw, hw, scale),
        out_shape=out_shape,
        in_specs=[spec] * 8,
        out_specs=[spec] * 6,
        scratch_shapes=scratch,
        compiler_params=pltpu.CompilerParams(
            collective_id=0, has_side_effects=True, vmem_limit_bytes=60 * 1024 * 1024),
    )(inputs, cotangent, *weights, slot, cols)
    anywhere = pl.BlockSpec(memory_space=pl.ANY)
    return tuple(pl.pallas_call(
        hand_on,
        out_shape=out_shape,
        in_specs=[anywhere] * 6,
        out_specs=[anywhere] * 6,
        scratch_shapes=[dma((6,))],
    )(*results))


def solution(mesh):
    def pick(*args):
        inputs, w_first, w_third = args[0], args[2], args[4]
        ranks, dps = mesh.shape["tensor"], mesh.shape["dp"]
        nblk, bw = w_first.shape[:2]
        aligned = (
            dps == 8 and nblk % 4 == 0 and bw // (nblk * ranks) == 8
            and (bw // dps) % 16 == 0 and (w_third.shape[1] // dps) % 16 == 0
            and (bw // ranks) % 16 == 0 and inputs.shape[0] % 128 == 0
        )
        return (fused_body if aligned else body)(*args)

    return jax.shard_map(
        pick,
        mesh=mesh,
        in_specs=(
            P("dp", "tensor"),
            P("dp", "tensor"),
            P("tensor", None, None),
            P("tensor", None, None),
            P("tensor", None, None),
            P("tensor", None, None),
            P(),
            P(),
        ),
        out_specs=(
            P("dp", "tensor"),
            P("dp", "tensor"),
            P("tensor", "dp", None),
            P("tensor", "dp", None),
            P("tensor", "dp", None),
            P("tensor", "dp", None),
        ),
        check_vma=False,
    )
```

```python
import functools
import math

import jax
import jax.numpy as jnp
from jax import lax
from jax.experimental import pallas as pl
from jax.experimental.pallas import tpu as pltpu
from jax.sharding import PartitionSpec as P


def blocks(z, w):
    rows = z.shape[0]
    nblk, fin, fout = w.shape
    out = jnp.einsum(
        "tli,lio->tlo", z.reshape(rows, nblk, fin), w, preferred_element_type=jnp.float32
    )
    return out.reshape(rows, nblk * fout)


def blocks_back(g, w):
    rows = g.shape[0]
    nblk, fin, fout = w.shape
    out = jnp.einsum(
        "tlo,lio->tli", g.reshape(rows, nblk, fout), w, preferred_element_type=jnp.float32
    )
    return out.reshape(rows, nblk * fin)


def block_grad(z, g, nblk, scale):
    rows = z.shape[0]
    total = jnp.einsum(
        "tli,tlo->lio",
        z.reshape(rows, nblk, -1),
        g.reshape(rows, nblk, -1),
        preferred_element_type=jnp.float32,
    )
    return total * scale


def gelu_tanh(v):
    return jax.nn.gelu(v, approximate=True)


def route_tables(route_all, width, ranks, rank):
    pieces = width // ranks
    grid = route_all.reshape(ranks, width)
    owner = grid // width
    local_col = grid - owner * width
    owner_hot = owner[:, :, None] == jnp.arange(ranks, dtype=jnp.int32)[None, None, :]
    counted = jnp.cumsum(owner_hot.astype(jnp.int32), axis=1)
    position = jnp.sum(jnp.where(owner_hot, counted, 0), axis=2) - 1
    recv_slot = owner * pieces + position
    my_slots = lax.dynamic_index_in_dim(recv_slot, rank, axis=0, keepdims=False)
    lanes = jnp.arange(width, dtype=jnp.int32)
    place_mat = (lanes[:, None] == my_slots[None, :]).astype(jnp.bfloat16)
    send_slot = (jnp.arange(ranks, dtype=jnp.int32)[:, None] * pieces + position).reshape(-1)
    owned = (owner == rank).reshape(-1)
    flat_col = local_col.reshape(-1)
    picks = jnp.logical_and(owned[None, :], send_slot[None, :] == lanes[:, None])
    col_of_slot = jnp.sum(jnp.where(picks, flat_col[None, :], 0), axis=1)
    send_mat = (lanes[:, None] == col_of_slot[None, :]).astype(jnp.bfloat16)
    return (send_mat, place_mat)


def apply_perm(x, table):
    return jnp.dot(x, table, preferred_element_type=jnp.float32).astype(jnp.bfloat16)


def apply_back(x, table):
    return lax.dot_general(
        x, table, (((1,), (1,)), ((), ())), preferred_element_type=jnp.float32
    ).astype(jnp.bfloat16)


def body(inputs, cotangent, w_first, w_second, w_third, w_fourth, route_up, route_down):
    ranks = lax.axis_size("tensor")
    rank = lax.axis_index("tensor")
    tok = inputs.shape[0]
    width = inputs.shape[1]
    pieces = width // ranks
    nblk = w_first.shape[0]
    scale = 1.0 / math.sqrt(tok * lax.axis_size("dp"))
    up_send, up_place = route_tables(route_up, width, ranks, rank)
    down_send, down_place = route_tables(route_down, width, ranks, rank)
    first_act = blocks(inputs, w_first).astype(jnp.bfloat16)
    outgoing = apply_perm(first_act, up_send).reshape(tok, ranks, pieces)
    received = lax.all_to_all(outgoing, "tensor", split_axis=1, concat_axis=1, tiled=True)
    mixed = apply_perm(received.reshape(received.shape[0], width), up_place)
    mixed_up = mixed
    pre_act = blocks(mixed, w_second).astype(jnp.bfloat16)
    pre_float = pre_act.astype(jnp.float32)
    hidden_act = gelu_tanh(pre_float).astype(jnp.bfloat16)
    third_act = blocks(hidden_act, w_third).astype(jnp.bfloat16)
    outgoing = apply_perm(third_act, down_send).reshape(tok, ranks, pieces)
    received = lax.all_to_all(outgoing, "tensor", split_axis=1, concat_axis=1, tiled=True)
    mixed = apply_perm(received.reshape(received.shape[0], width), down_place)
    layer_out = blocks(mixed, w_fourth).astype(jnp.bfloat16)
    back_mixed_down = blocks_back(cotangent, w_fourth).astype(jnp.bfloat16)
    grad_fourth = block_grad(mixed, cotangent, nblk, scale)
    returning = apply_back(back_mixed_down, down_place).reshape(tok, ranks, pieces)
    received = lax.all_to_all(returning, "tensor", split_axis=1, concat_axis=1, tiled=True)
    back = apply_back(received.reshape(received.shape[0], width), down_send)
    back_third = back
    back_hidden = blocks_back(back, w_third)
    grad_third = block_grad(hidden_act, back_third, nblk, scale)
    pull = jax.vjp(gelu_tanh, pre_float)[1]
    back_pre = pull(back_hidden)[0].astype(jnp.bfloat16)
    grad_second = block_grad(mixed_up, back_pre, nblk, scale)
    back_mixed_up = blocks_back(back_pre, w_second).astype(jnp.bfloat16)
    returning = apply_back(back_mixed_up, up_place).reshape(tok, ranks, pieces)
    received = lax.all_to_all(returning, "tensor", split_axis=1, concat_axis=1, tiled=True)
    back = apply_back(received.reshape(received.shape[0], width), up_send)
    grad_input = blocks_back(back, w_first).astype(jnp.bfloat16)
    grad_first = block_grad(inputs, back, nblk, scale)
    def shared(total):
        return lax.psum_scatter(
            total.astype(jnp.bfloat16), "dp", scatter_dimension=1, tiled=True
        ).astype(jnp.float32)

    return (
        layer_out, grad_input, shared(grad_first), shared(grad_second),
        shared(grad_third), shared(grad_fourth),
    )


MESH = pl.DeviceIdType.MESH
NN = (((1,), (0,)), ((), ()))
NT = (((1,), (1,)), ((), ()))
TN = (((0,), (0,)), ((), ()))
GELU_C = 0.7978845608
GELU_A = 0.044715


def mm(a, b, dims):
    return lax.dot_general(a, b, dims, preferred_element_type=jnp.float32)


def route_slots(routes, nb, ranks, rank):
    bw = routes.shape[-1]
    share = bw // nb
    nblk = nb // ranks
    src = routes // bw
    col = routes - src * bw
    hot = src[:, :, None, :] == jnp.arange(nb, dtype=jnp.int32)[None, None, :, None]
    upto = jnp.arange(bw)[:, None] <= jnp.arange(bw)[None, :]
    counted = jnp.einsum(
        "zbsk,kl->zbsl",
        hot.astype(jnp.bfloat16),
        upto.astype(jnp.bfloat16),
        preferred_element_type=jnp.float32,
    )
    j = jnp.sum(jnp.where(hot, counted, 0.0), axis=2).astype(jnp.int32) - 1
    slot = src * share + j
    mine = lax.dynamic_slice_in_dim(slot, rank * nblk, nblk, 1)
    local = slot - rank * (nblk * share)
    m = jnp.arange(nblk * share, dtype=jnp.int32)[None, None, :, None]
    cols = jnp.sum(jnp.where(local[:, :, None, :] == m, col[:, :, None, :], 0), axis=3)
    cols = cols.reshape(2, nb, nblk, share).transpose(0, 1, 3, 2).reshape(2, bw, nblk)
    return mine, cols


def layer_kernel(ranks, nblk, tok, bw, hw, scale, inp, cot, w1, w2, w3, w4, slot, cols,
                 out, gin, o1, o2, o3, o4,
                 pmat, smat, act, mup, mdn, bth, bfs, pre, hid, bpr, stage, sbuf, rbuf,
                 g1, g2, g3, g4, a1, a2, a3, a4, b1, b2, b3, b4, c1, c2, c3, c4,
                 ssem, rsem, asend, arecv, bsend, brecv, csend, crecv):
    bf = jnp.bfloat16
    rank = lax.axis_index("tensor")
    dp = lax.axis_index("dp")
    core = dp % 2
    x = (dp // 2) % 2
    y = dp // 4
    to_core = dp + 1 - 2 * core
    to_x = dp + 2 - 4 * x
    to_y = dp + 4 - 8 * y
    share = bw // (nblk * ranks)
    part = nblk * share
    hb = nblk // 2
    quarter = hb // 2
    gs, ras, rbs, rcs, outs = (g1, g2, g3, g4), (a1, a2, a3, a4), (b1, b2, b3, b4), (c1, c2, c3, c4), (o1, o2, o3, o4)

    barrier = pltpu.get_barrier_semaphore()
    for k in range(1, ranks):
        pl.semaphore_signal(barrier, inc=1, device_id=(dp, (rank + k) % ranks), device_id_type=MESH)
    for peer in (to_core, to_x, to_y):
        pl.semaphore_signal(barrier, inc=1, device_id=(peer, rank), device_id_type=MESH)

    lane = lax.broadcasted_iota(jnp.int32, (bw, bw), 1)
    row = lax.broadcasted_iota(jnp.int32, (bw, bw), 0)

    def make_smat(z):
        for s in range(nblk):
            smat[z, s] = (cols[z, :, s:s + 1] == lane).astype(jnp.float32).astype(bf)

    def make_pmat(z):
        for d in range(nblk):
            pmat[z, d] = (slot[z, d:d + 1, :] == row).astype(jnp.float32).astype(bf)

    def blk(b):
        return pl.ds(pl.multiple_of(b * bw, bw), bw)

    def each(step, c=None):
        def one(b, carry):
            step(b)
            return carry
        lax.fori_loop(*((0, nblk) if c is None else (c * hb, c * hb + hb)), one, 0)

    def piece(e, c):
        if e in (0, 3):
            return pl.ds(c * hb, hb), slice(None)
        return slice(None), pl.ds(c * hb * share, hb * share)

    def hop(e, c, k):
        peer = (rank + k) % ranks
        rows, cut = piece(e, c)
        return pltpu.make_async_remote_copy(
            src_ref=sbuf.at[e, peer, rows, cut], dst_ref=rbuf.at[e, rank, rows, cut],
            send_sem=ssem.at[e, c, k - 1], recv_sem=rsem.at[e, c, k - 1],
            device_id=(dp, peer), device_id_type=MESH)

    def send(e, c):
        for k in (2, 1, 3) if ranks == 4 else range(1, ranks):
            hop(e, c, k).start()
        rows, cut = piece(e, c)
        rbuf[e, rank, rows, cut] = sbuf[e, rank, rows, cut]

    def arrive(e, c):
        for k in range(1, ranks):
            hop(e, c, k).wait_recv()

    def sort_out(z, b, value):
        rows = mm(smat[z, b], value, NT).reshape(ranks, nblk, share, tok)
        stage[:, :, pl.ds(pl.multiple_of(b * share, share), share), :] = rows

    def placed(e, z, b):
        return mm(rbuf[e, :, b].reshape(bw, tok), pmat[z, b], TN).astype(bf)

    def unplace(e, z, b, value):
        sbuf[e, :, b] = mm(pmat[z, b], value, NT).astype(bf).reshape(ranks, part, tok)

    def unsorted(z, b):
        rows = stage[:, :, pl.ds(pl.multiple_of(b * share, share), share), :]
        return mm(rows.reshape(bw, tok).astype(bf), smat[z, b], TN).astype(bf)

    def put_grad(w, b, left, right):
        term = (mm(left, right, TN) * scale).astype(bf)
        gs[w][:, :, :, b] = term.reshape((2, 2, 2) + gs[w].shape[4:])

    def copy_a(w, c):
        return pltpu.make_async_remote_copy(
            src_ref=gs[w].at[:, :, 1 - core, pl.ds(c * hb, hb)],
            dst_ref=ras[w].at[:, :, pl.ds(c * hb, hb)],
            send_sem=asend.at[w, c], recv_sem=arecv.at[w, c],
            device_id=(to_core, rank), device_id_type=MESH)

    def spans(c):
        return pl.ds(c * hb, quarter), pl.ds(c * hb + quarter, quarter)

    def copies_b(w, c):
        lo, hi = spans(c)
        return (
            pltpu.make_async_remote_copy(
                src_ref=ras[w].at[:, 1 - x, lo], dst_ref=rbs[w].at[:, lo],
                send_sem=bsend.at[w, c, 0], recv_sem=brecv.at[w, c, 0],
                device_id=(to_x, rank), device_id_type=MESH),
            pltpu.make_async_remote_copy(
                src_ref=ras[w].at[1 - y, :, hi], dst_ref=rbs[w].at[:, hi],
                send_sem=bsend.at[w, c, 1], recv_sem=brecv.at[w, c, 1],
                device_id=(to_y, rank), device_id_type=MESH))

    def copies_c(w, c):
        lo, hi = spans(c)
        return (
            pltpu.make_async_remote_copy(
                src_ref=rbs[w].at[1 - y, lo], dst_ref=rcs[w].at[lo],
                send_sem=csend.at[w, c, 0], recv_sem=crecv.at[w, c, 0],
                device_id=(to_y, rank), device_id_type=MESH),
            pltpu.make_async_remote_copy(
                src_ref=rbs[w].at[1 - x, hi], dst_ref=rcs[w].at[hi],
                send_sem=csend.at[w, c, 1], recv_sem=crecv.at[w, c, 1],
                device_id=(to_x, rank), device_id_type=MESH))

    def f32(v):
        return v.astype(jnp.float32)

    def a_to_b(w, c):
        copy_a(w, c).wait_recv()

        def step(b):
            ras[w][:, :, b] = (f32(ras[w][:, :, b]) + f32(gs[w][:, :, core, b])).astype(bf)
        each(step, c)
        for copy in copies_b(w, c):
            copy.start()

    def b_to_c(w, c):
        for copy in copies_b(w, c):
            copy.wait_recv()

        def one(b, carry):
            rbs[w][:, b] = (f32(rbs[w][:, b]) + f32(ras[w][:, x, b])).astype(bf)
            h = b + quarter
            rbs[w][:, h] = (f32(rbs[w][:, h]) + f32(ras[w][y, :, h])).astype(bf)
            return carry
        lax.fori_loop(c * hb, c * hb + quarter, one, 0)
        for copy in copies_c(w, c):
            copy.start()

    def finish(w, c):
        for copy in copies_c(w, c):
            copy.wait_recv()

        def one(b, carry):
            h = b + quarter
            outs[w][b] = f32(rbs[w][y, b]) + f32(rcs[w][b])
            outs[w][h] = f32(rbs[w][x, h]) + f32(rcs[w][h])
            return carry
        lax.fori_loop(c * hb, c * hb + quarter, one, 0)

    make_smat(0)

    def first(b):
        sort_out(0, b, mm(inp[:, blk(b)], w1[b], NN).astype(bf))
    each(first)
    pl.semaphore_wait(barrier, ranks - 1 + 3)
    sbuf[0] = stage[...].astype(bf)
    send(0, 0)

    make_pmat(1)

    def back_fourth(b):
        unplace(1, 1, b, mm(cot[:, blk(b)], w4[b], NT).astype(bf))
    each(back_fourth)
    send(1, 0)
    make_pmat(0)
    make_smat(1)

    def middle(b):
        m = placed(0, 0, b)
        mup[b] = m
        p = mm(m, w2[b], NN).astype(bf)
        pre[b] = p
        v = f32(p)
        h = (0.5 * v * (1.0 + jnp.tanh(GELU_C * (v + GELU_A * (v * v * v))))).astype(bf)
        hid[b] = h
        sort_out(1, b, mm(h, w3[b], NN).astype(bf))
    def load(e, c):
        rows, cut = piece(e, c)
        stage[:, rows, cut] = f32(rbuf[e, :, rows, cut])

    def forward(c):
        each(middle, c)
        rows, cut = piece(2, c)
        sbuf[2, :, rows, cut] = stage[:, rows, cut].astype(bf)

    def third(b):
        t = unsorted(1, b)
        bth[b] = t
        put_grad(2, b, hid[b], t)

    def back_second(b):
        v = f32(pre[b])
        v2 = v * v
        th = jnp.tanh(GELU_C * (v + GELU_A * (v2 * v)))
        slope = 0.5 * (1.0 + th) + 0.5 * v * (1.0 - th * th) * (GELU_C * (1.0 + 3.0 * GELU_A * v2))
        p = (mm(bth[b], w3[b], NT) * slope).astype(bf)
        bpr[b] = p
        unplace(3, 0, b, mm(p, w2[b], NT).astype(bf))
    def second(b):
        put_grad(1, b, mup[b], bpr[b])

    def fourth(b):
        m = placed(2, 1, b)
        out[:, blk(b)] = mm(m, w4[b], NN).astype(bf)
        put_grad(3, b, m, cot[:, blk(b)])
    def last(b):
        t = unsorted(0, b)
        put_grad(0, b, inp[:, blk(b)], t)
        gin[:, blk(b)] = mm(t, w1[b], NT).astype(bf)

    arrive(0, 0)
    send(0, 1)
    forward(0)
    arrive(1, 0)
    send(1, 1)
    load(1, 0)
    each(third, 0)
    copy_a(2, 0).start()
    each(back_second, 0)
    a_to_b(2, 0)
    each(second, 0)
    copy_a(1, 0).start()

    arrive(0, 1)
    send(2, 0)
    forward(1)
    a_to_b(1, 0)
    arrive(1, 1)
    send(2, 1)
    send(3, 0)
    load(1, 1)
    each(third, 1)
    copy_a(2, 1).start()
    each(back_second, 1)
    send(3, 1)
    a_to_b(2, 1)
    each(second, 1)
    copy_a(1, 1).start()
    b_to_c(2, 0)
    a_to_b(1, 1)
    b_to_c(1, 0)

    for c in range(2):
        arrive(2, c)
    for c in range(2):
        each(fourth, c)
        copy_a(3, c).start()
    for c in range(2):
        a_to_b(3, c)
    b_to_c(2, 1)

    for c in range(2):
        arrive(3, c)
    stage[...] = f32(rbuf[3])
    for c in range(2):
        each(last, c)
        copy_a(0, c).start()
    for c in range(2):
        a_to_b(0, c)
    order = [(1, 1), (3, 0), (3, 1), (0, 0), (0, 1)]
    for w, c in order:
        b_to_c(w, c)
    for w, c in [(2, 0), (1, 0), (2, 1)] + order:
        finish(w, c)

    for c in range(2):
        for e in range(4):
            for k in range(1, ranks):
                hop(e, c, k).wait_send()
        for w in range(4):
            copy_a(w, c).wait_send()
            for copy in copies_b(w, c) + copies_c(w, c):
                copy.wait_send()


def hand_on(*refs):
    n = (len(refs) - 2) // 3
    arrived, left = refs[3 * n:]
    held = refs[2 * n:3 * n]
    loads = [pltpu.make_async_copy(refs[i], held[i], arrived.at[i]) for i in range(n)]
    stores = [pltpu.make_async_copy(held[i], refs[n + i], left.at[i]) for i in range(n)]
    for load in loads:
        load.start()
    for load, store in zip(loads, stores):
        load.wait()
        store.start()
    for store in stores:
        store.wait()


def fused_body(inputs, cotangent, w_first, w_second, w_third, w_fourth, route_up, route_down):
    ranks = lax.axis_size("tensor")
    dps = lax.axis_size("dp")
    rank = lax.axis_index("tensor")
    tok, width = inputs.shape
    nblk, bw, hw = w_second.shape
    nb = nblk * ranks
    part = bw // ranks
    scale = 1.0 / math.sqrt(tok * dps)
    routes = jnp.stack([route_up, route_down]).reshape(2, nb, bw)
    slot, cols = route_slots(routes, nb, ranks, rank)
    weights = (w_first, w_second, w_third, w_fourth)
    shapes = [(w.shape[1] // dps, w.shape[2]) for w in weights]
    bf = jnp.bfloat16
    vm = pltpu.VMEM
    scratch = [
        vm((2, nblk, bw, bw), bf), vm((2, nblk, bw, bw), bf),
        vm((nblk, tok, bw), bf), vm((nblk, tok, bw), bf), vm((nblk, tok, bw), bf),
        vm((nblk, tok, bw), bf), vm((nblk, tok, bw), bf),
        vm((nblk, tok, hw), bf), vm((nblk, tok, hw), bf), vm((nblk, tok, hw), bf),
        vm((ranks, nblk, part, tok), jnp.float32),
        vm((4, ranks, nblk, part, tok), bf), vm((4, ranks, nblk, part, tok), bf),
    ]
    scratch += [vm((2, 2, 2, nblk) + s, bf) for s in shapes]
    scratch += [vm((2, 2, nblk) + s, bf) for s in shapes]
    scratch += [vm((2, nblk) + s, bf) for s in shapes]
    scratch += [vm((nblk,) + s, bf) for s in shapes]
    dma = pltpu.SemaphoreType.DMA
    scratch += [dma((4, 2, ranks - 1))] * 2 + [dma((4, 2))] * 2
    scratch += [dma((4, 2, 2))] * 4
    out_shape = [jax.ShapeDtypeStruct((tok, width), bf)] * 2
    out_shape += [jax.ShapeDtypeStruct((nblk,) + s, jnp.float32) for s in shapes]
    spec = pl.BlockSpec(memory_space=pltpu.VMEM)
    results = pl.pallas_call(
        functools.partial(layer_kernel, ranks, nblk, tok, bw, hw, scale),
        out_shape=out_shape,
        in_specs=[spec] * 8,
        out_specs=[spec] * 6,
        scratch_shapes=scratch,
        compiler_params=pltpu.CompilerParams(
            collective_id=0, has_side_effects=True, vmem_limit_bytes=60 * 1024 * 1024),
    )(inputs, cotangent, *weights, slot, cols)
    anywhere = pl.BlockSpec(memory_space=pl.ANY)
    return tuple(pl.pallas_call(
        hand_on,
        out_shape=out_shape,
        in_specs=[anywhere] * 6,
        out_specs=[anywhere] * 6,
        scratch_shapes=[vm(o.shape, o.dtype) for o in out_shape] + [dma((6,)), dma((6,))],
        compiler_params=pltpu.CompilerParams(vmem_limit_bytes=32 * 1024 * 1024),
    )(*results))


def solution(mesh):
    def pick(*args):
        inputs, w_first, w_third = args[0], args[2], args[4]
        ranks, dps = mesh.shape["tensor"], mesh.shape["dp"]
        nblk, bw = w_first.shape[:2]
        aligned = (
            dps == 8 and nblk % 4 == 0 and bw // (nblk * ranks) == 8
            and (bw // dps) % 16 == 0 and (w_third.shape[1] // dps) % 16 == 0
            and (bw // ranks) % 16 == 0 and inputs.shape[0] % 128 == 0
        )
        return (fused_body if aligned else body)(*args)

    return jax.shard_map(
        pick,
        mesh=mesh,
        in_specs=(
            P("dp", "tensor"),
            P("dp", "tensor"),
            P("tensor", None, None),
            P("tensor", None, None),
            P("tensor", None, None),
            P("tensor", None, None),
            P(),
            P(),
        ),
        out_specs=(
            P("dp", "tensor"),
            P("dp", "tensor"),
            P("tensor", "dp", None),
            P("tensor", "dp", None),
            P("tensor", "dp", None),
            P("tensor", "dp", None),
        ),
        check_vma=False,
    )
```
